32 devices in a mesh: groups: 2 (over y), row: 4 (over z), col: 2 (over x), sub: 2 (over core).
Axes of the slice: x: 2, y: 2, z: 4, core: 2. Of those that a mesh axis runs over, the one named last changes fastest.
Arguments:
- alignment: bfloat16 [64, 128, 256], P(('groups', 'row', 'col')), parts along dimension 0, may hold values from -12 to 12, as said below
- alignment_mask: int32 [64, 128], P(('groups', 'row', 'col')), parts along dimension 0, may hold values from 0 to 1
- residue_mask: int32 [256], P('groups'), parts along dimension 0, may hold values 0 or 1
- pair_state: bfloat16 [256, 128, 128], P(('groups', 'row'), ('col', 'sub')), parts along dimension 0, may hold values from -8 to 8
- alignment_gain: float32 [256], replicated, may hold values from 0.1 to 1.9
- alignment_offset: float32 [256], replicated, may hold values from -3 to 3
- left_weight: bfloat16 [256, 32], replicated, may hold values from -0.375 to 0.375
- left_offset: float32 [32], replicated, may hold values from -3 to 3
- right_weight: bfloat16 [256, 32], replicated, may hold values from -0.375 to 0.375
- right_offset: float32 [32], replicated, may hold values from -3 to 3
- out_weight: bfloat16 [32, 32, 128], replicated, may hold values from -0.1875 to 0.1875
- out_offset: float32 [128], replicated, may hold values from -3 to 3
- pair_gain: float32 [128], replicated, may hold values from 0.1 to 1.9
- pair_offset: float32 [128], replicated, may hold values from -3 to 3
Outputs:
- new_pair: bfloat16 [256, 128, 128], P(('groups', 'row'), ('col', 'sub')), parts along dimension 0
The draws below stay inside these ranges and needn't reach their ends.
There are 2 independent parts, one for each index of `groups`. The reference program is written for one: setup_inputs(seed, part) draws one part's arguments, and reference() takes and returns one part's arrays. A program takes and returns all parts, laid end to end along the dimension named above; an argument that names none is the same for every part. Nothing has to cross between parts.
Inputs may be any that keep to these rules, and one draw needn't show every extreme that they name: `alignment`: whole rows of the representation, with spread channel scales.
All inputs are finite; a program needn't handle non-finite values.
Results may differ from the reference program's by a relative error of at most 0.0053.
Values may be sent and summed in bfloat16 or wider, within the bound.
A program may use at most 128 MiB of HBM per device.

```python
import jax
import jax.numpy as jnp
from jax import lax

CM = 256
HID = 32
CZ = 128
RI = 32
S = 32
R = 128
N_ROW = 4


def draw_alignment(key, part):
    key = jax.random.fold_in(key, 11)
    channel_scale = jnp.exp(jax.random.uniform(jax.random.fold_in(key, 1), (1, 1, CM), minval=-1.15, maxval=1.15))
    row_scale = jnp.exp(jax.random.uniform(jax.random.fold_in(key, 2), (S, R, 1), minval=-1.15, maxval=1.15))
    values = jax.random.normal(jax.random.fold_in(key, 3), (S, R, CM))
    return jnp.clip(values * channel_scale * row_scale, -12.0, 12.0).astype(jnp.bfloat16)


def draw_alignment_mask(key, part):
    key = jax.random.fold_in(key, 23)
    starts = jax.random.randint(jax.random.fold_in(key, 1), (S, 1), 0, R)
    spans = jax.random.randint(jax.random.fold_in(key, 2), (S, 1), max(R // 8, 1), R + 1)
    position = jnp.arange(R, dtype=jnp.int32)[None, :]
    inside = (position >= starts) & (position < starts + spans)
    kept = jax.random.randint(jax.random.fold_in(key, 3), (S, R), 0, 8) > 0
    query_row = jnp.arange(S, dtype=jnp.int32)[:, None] == 0
    return jnp.where(query_row, 1, (inside & kept).astype(jnp.int32)).astype(jnp.int32)


def draw_pair_state(key, part):
    key = jax.random.fold_in(key, 37)
    channel_scale = 0.4 * jnp.exp(jax.random.uniform(jax.random.fold_in(key, 1), (1, 1, CZ), minval=-1.15, maxval=1.15))
    values = jax.random.normal(jax.random.fold_in(key, 2), (R, R, CZ)) * channel_scale
    return jnp.clip(values, -8.0, 8.0).astype(jnp.bfloat16)


def set_ends(drawn, own_key, low, top_value):
    index_at = [jax.random.randint(jax.random.fold_in(own_key, axis), (), 0, length) for axis, length in enumerate(drawn.shape)]
    main_axis = drawn.shape.index(max(drawn.shape))
    next_to = index_at[:main_axis] + [(index_at[main_axis] + 1) % drawn.shape[main_axis]] + index_at[main_axis + 1:]
    return drawn.at[tuple(index_at)].set(low).at[tuple(next_to)].set(top_value)


def noise(rng, dims, deviation, limit, kind=jnp.bfloat16):
    return jnp.clip(deviation * jax.random.normal(rng, dims, jnp.float32), -limit, limit).astype(kind)


def setup_inputs(seed: int = 0, part: int = 0) -> dict:
    keys = jax.random.split(jax.random.key(seed), 15)
    own_keys = jax.random.split(jax.random.fold_in(keys[14], part), 15)
    return {
        "alignment": draw_alignment(jax.random.fold_in(jax.random.fold_in(keys[14], part), 71), part),
        "alignment_mask": draw_alignment_mask(jax.random.fold_in(jax.random.fold_in(keys[14], part), 71), part),
        "residue_mask": set_ends((jax.random.randint(own_keys[2], (R,), 0, 8) < 7).astype(jnp.int32), jax.random.fold_in(own_keys[2], 1), 0, 1),
        "pair_state": draw_pair_state(jax.random.fold_in(jax.random.fold_in(keys[14], part), 71), part),
        "alignment_gain": jnp.clip(1.0 + 0.18 * jax.random.normal(keys[4], (CM,), jnp.float32), 0.1, 1.9),
        "alignment_offset": noise(keys[5], (CM,), 0.5, 3.0, jnp.float32),
        "left_weight": noise(keys[6], (CM, HID), CM ** -0.5, 0.375),
        "left_offset": noise(keys[7], (HID,), 0.5, 3.0, jnp.float32),
        "right_weight": noise(keys[8], (CM, HID), CM ** -0.5, 0.375),
        "right_offset": noise(keys[9], (HID,), 0.5, 3.0, jnp.float32),
        "out_weight": noise(keys[10], (HID, HID, CZ), (HID * HID) ** -0.5, 0.1875),
        "out_offset": noise(keys[11], (CZ,), 0.5, 3.0, jnp.float32),
        "pair_gain": jnp.clip(1.0 + 0.18 * jax.random.normal(keys[12], (CZ,), jnp.float32), 0.1, 1.9),
        "pair_offset": noise(keys[13], (CZ,), 0.5, 3.0, jnp.float32),
    }


def normalize(values, scales, offsets):
    average = lax.optimization_barrier(jnp.mean(values, axis=-1, keepdims=True))
    variance = lax.optimization_barrier(jnp.mean(values * values, axis=-1, keepdims=True)) - average * average
    return (values - average) * lax.rsqrt(variance + 1e-05) * scales + offsets

def reference(alignment, alignment_mask, residue_mask, pair_state, alignment_gain, alignment_offset, left_weight, left_offset, right_weight, right_offset, out_weight, out_offset, pair_gain, pair_offset):
    present = (alignment_mask * residue_mask[None, :]).astype(jnp.bfloat16)
    factor = present.astype(jnp.float32)[:, :, None]
    normed = normalize(alignment.astype(jnp.float32), alignment_gain, alignment_offset).astype(jnp.bfloat16)
    flattened = normed.reshape(S * R, CM)
    left_side = ((jnp.dot(flattened, left_weight, preferred_element_type=jnp.float32).reshape(S, R, HID) + left_offset) * factor).astype(jnp.bfloat16)
    right_side = ((jnp.dot(flattened, right_weight, preferred_element_type=jnp.float32).reshape(S, R, HID) + right_offset) * factor).astype(jnp.bfloat16)
    counts = jnp.dot(present.T, present, preferred_element_type=jnp.float32)
    out_flat = out_weight.reshape(HID * HID, CZ)
    right_wide = right_side.astype(jnp.float32)

    def one_block(block_index):
        first_row = (block_index * RI).astype(jnp.int32)
        row_values = lax.dynamic_slice_in_dim(left_side, first_row, RI, 1).astype(jnp.float32)
        products = jnp.einsum('sic,sje->ijce', row_values, right_wide).astype(jnp.bfloat16)
        projected = jnp.dot(products.reshape(RI * R, HID * HID), out_flat, preferred_element_type=jnp.float32).reshape(RI, R, CZ) + out_offset
        row_counts = lax.dynamic_slice_in_dim(counts, first_row, RI, 0)
        update = projected / jnp.maximum(row_counts, 1.0)[:, :, None]
        summed = lax.dynamic_slice_in_dim(pair_state, first_row, RI, 0).astype(jnp.float32) + update
        return normalize(summed, pair_gain, pair_offset).astype(jnp.bfloat16)
    blocks = lax.map(one_block, jnp.arange(N_ROW, dtype=jnp.int32))
    return blocks.reshape(R, R, CZ)
```

```python
import functools

import jax
import jax.numpy as jnp
from jax import lax
from jax.experimental import pallas as pl
from jax.experimental.pallas import tpu as pltpu
from jax.sharding import PartitionSpec as P


def normalize(values, scales, offsets):
    average = jnp.mean(values, axis=-1, keepdims=True)
    variance = jnp.mean(values * values, axis=-1, keepdims=True) - average * average
    return (values - average) * lax.rsqrt(variance + 1e-05) * scales + offsets


def project_side(normed, weight, offsets, factor):
    leading = normed.shape[:-1]
    flattened = jnp.dot(
        normed.reshape(-1, normed.shape[-1]), weight, preferred_element_type=jnp.float32
    )
    return ((flattened.reshape(leading + (weight.shape[1],)) + offsets) * factor[..., None]).astype(
        jnp.bfloat16
    )


def reorder(values, row_count, col_count, sub_count):
    local_seqs = values.shape[0]
    portion = values.shape[1] // (row_count * col_count * sub_count)
    trailing = values.shape[2:]
    grouped = values.reshape((local_seqs, col_count, sub_count, row_count, portion) + trailing)
    extra = tuple(range(5, 5 + len(trailing)))
    return jnp.transpose(grouped, (0, 3, 1, 2, 4) + extra).reshape(values.shape)


def own_half(values, sub_count, sub_index):
    sequences = values.shape[0]
    share = values.shape[1] // sub_count
    split = values.reshape((sequences, sub_count, share) + values.shape[2:])
    picked = lax.dynamic_slice_in_dim(split, sub_index, 1, 1)
    return picked.reshape((sequences, share) + values.shape[2:])


def column_terms(left_rows, row_mask, right_cols, col_mask, out_flat, out_offset):
    col_total = right_cols.shape[1]
    results = []
    for first_col in range(0, col_total, 32):
        last_col = min(first_col + 32, col_total)
        selected = right_cols[:, first_col:last_col]
        products = jnp.einsum(
            "sic,sje->ijce", left_rows, selected, preferred_element_type=jnp.float32
        ).astype(jnp.bfloat16)
        pair_rows = products.shape[0] * products.shape[1]
        projected = jnp.dot(
            products.reshape(pair_rows, -1), out_flat, preferred_element_type=jnp.float32
        )
        projected = projected.reshape(products.shape[0], products.shape[1], -1) + out_offset
        counts = jnp.dot(
            row_mask.T, col_mask[:, first_col:last_col], preferred_element_type=jnp.float32
        )
        results.append(projected / jnp.maximum(counts, 1.0)[:, :, None])
    return jnp.concatenate(results, axis=1)


def body(
    alignment,
    alignment_mask,
    residue_mask,
    pair_state,
    alignment_gain,
    alignment_offset,
    left_weight,
    left_offset,
    right_weight,
    right_offset,
    out_weight,
    out_offset,
    pair_gain,
    pair_offset,
):
    row_count = lax.axis_size("row")
    col_count = lax.axis_size("col")
    sub_count = lax.axis_size("sub")
    sub_index = lax.axis_index("sub")
    local_seqs, residues, channels = alignment.shape
    hidden = left_weight.shape[1]
    portion = residues // (row_count * col_count)
    present = (alignment_mask * residue_mask[None, :]).astype(jnp.bfloat16)
    normed = normalize(alignment.astype(jnp.float32), alignment_gain, alignment_offset).astype(
        jnp.bfloat16
    )
    factor = present.astype(jnp.float32)
    left_local = project_side(normed, left_weight, left_offset, factor)
    right_local = reorder(
        project_side(normed, right_weight, right_offset, factor), row_count, col_count, sub_count
    )
    outgoing = (
        left_local.reshape(local_seqs, -1),
        right_local.reshape(local_seqs, -1),
        present,
        reorder(present, row_count, col_count, sub_count),
    )
    arrived = (
        lax.all_to_all(outgoing[0], ("row", "col"), split_axis=1, concat_axis=0, tiled=True),
        lax.all_to_all(outgoing[1], ("row", "col"), split_axis=1, concat_axis=0, tiled=True),
        lax.all_to_all(outgoing[2], ("row", "col"), split_axis=1, concat_axis=0, tiled=True),
        lax.all_to_all(outgoing[3], ("row", "col"), split_axis=1, concat_axis=0, tiled=True),
    )
    sequences = arrived[2].shape[0]
    left_part = arrived[0].reshape(sequences, portion, hidden)
    right_part = own_half(arrived[1].reshape(sequences, portion, hidden), sub_count, sub_index)
    mask_here = arrived[2]
    mask_there = own_half(arrived[3], sub_count, sub_index)
    gathered_rows, row_mask = (
        lax.all_gather(left_part.reshape(sequences, -1), "col", axis=1, tiled=True),
        lax.all_gather(mask_here, "col", axis=1, tiled=True),
    )
    left_rows = gathered_rows.reshape(sequences, -1, hidden)
    out_flat = out_weight.reshape(hidden * hidden, -1)
    pieces = lax.all_gather((right_part, mask_there), "row", axis=1, tiled=True)
    update = column_terms(left_rows, row_mask, pieces[0], pieces[1], out_flat, out_offset)
    summed = pair_state.astype(jnp.float32) + update
    return normalize(summed, pair_gain, pair_offset).astype(jnp.bfloat16)


F32, BF16 = jnp.float32, jnp.bfloat16


def iota(shape, axis):
    return lax.broadcasted_iota(jnp.int32, shape, axis)


def one_hot(condition, kind=BF16):
    return jnp.where(condition, 1.0, 0.0).astype(kind)


def dot(a, b, **options):
    return jnp.dot(a, b, preferred_element_type=F32, **options)


def dot_nt(a, b):
    return lax.dot_general(a, b, (((1,), (1,)), ((), ())), preferred_element_type=F32)


def pair_kernel(
    row_count, col_count, sub_count,
    x_ref, am_ref, rm_ref, pair_ref, ag_ref, ao_ref, lw_ref, lo_ref, rw_ref, ro_ref,
    ow_ref, oo_ref, pg_ref, po_ref, out_ref,
    send, recv, right_buf, left_wide, w_buf, prod, ml_buf, cm_buf, send_sem, recv_sem,
):
    peers = row_count * col_count
    row, col, sub = lax.axis_index("row"), lax.axis_index("col"), lax.axis_index("sub")
    me = row * col_count + col
    barrier = pltpu.get_barrier_semaphore()
    others = []
    for k in range(1, peers):
        peer = lax.rem(me + k, peers)
        place = {"row": peer // col_count, "col": lax.rem(peer, col_count)}
        others.append((k, peer, place))
        pl.semaphore_signal(barrier, inc=1, device_id=place, device_id_type=pl.DeviceIdType.MESH)

    in_32, lane = iota((32, 128), 0), iota((32, 128), 1)
    rep_left = lane % 32 == in_32
    rep_right = (lane // 32) * 8 + lane % 8 == in_32
    wide = jnp.concatenate(
        [dot(lw_ref[...], one_hot(rep_left)), dot(rw_ref[...], one_hot(rep_right))], axis=1
    ).astype(BF16)
    exact = lax.Precision.HIGHEST
    bias = jnp.concatenate(
        [
            dot(jnp.broadcast_to(lo_ref[...], (8, 32)), one_hot(rep_left, F32), precision=exact),
            dot(jnp.broadcast_to(ro_ref[...], (8, 32)), one_hot(rep_right, F32), precision=exact),
        ],
        axis=1,
    )[0:1]
    present = (am_ref[...] * rm_ref[...]).astype(F32)
    at, seq_row = iota((256, 128), 0), None
    seq_row = jnp.where(at < 128, at // 32, (at // 8) % 4)
    mask_rows = jnp.zeros((256, 128), F32)
    for s in range(4):
        mask_rows = jnp.where(seq_row == s, present[s : s + 1], mask_rows)
    eye = one_hot(iota((128, 128), 0) == iota((128, 128), 1))
    mask_here = dot_nt(eye, mask_rows.astype(BF16))
    lane2 = iota((128, 256), 1)
    seq_lane = jnp.where(lane2 < 128, lane2 // 32, (lane2 // 8) % 4)
    sides = jnp.zeros((128, 256), F32)
    for s in range(4):
        normed = normalize(x_ref[s].astype(F32), ag_ref[...], ao_ref[...]).astype(BF16)
        sides = jnp.where(seq_lane == s, dot(normed, wide), sides)
    sides = ((sides + bias) * mask_here).astype(BF16)
    left = sides[:, :128]
    right_buf[...] = sides[:, 128:]
    mask_block = jnp.concatenate([present, jnp.zeros((12, 128), F32)], axis=0).astype(BF16)
    for d in range(peers):
        r, q = d // col_count, d % col_count
        send[d, 0:32] = left[r * 32 : r * 32 + 32]
        start = pl.multiple_of((q * sub_count + sub) * 32, 32)
        send[d, 32:64] = right_buf[pl.ds(start, 32)]
        send[d, 64:80] = mask_block

    pl.semaphore_wait(barrier, peers - 1)
    copies = []
    for k, peer, place in others:
        copy = pltpu.make_async_remote_copy(
            src_ref=send.at[peer],
            dst_ref=recv.at[me],
            send_sem=send_sem.at[k],
            recv_sem=recv_sem.at[k],
            device_id=place,
            device_id_type=pl.DeviceIdType.MESH,
        )
        copy.start()
        copies.append(copy)
    recv[me] = send[me]

    for eb in range(4):
        part = ow_ref[...].astype(F32)[:, eb * 8 : eb * 8 + 8, :]
        w_buf[eb] = part.reshape(256, 128).astype(BF16)
    a, b = iota((256, 256), 0), iota((256, 256), 1)
    swap_rows = one_hot((a % 8 == b // 32) & (a // 8 == b % 32))
    swap_lanes = one_hot((a // 32 == b % 8) & ((a // 8) % 4 == (b // 8) % 4) & (a % 8 == b // 32))
    a, b = iota((128, 1024), 0), iota((128, 1024), 1)
    spread = one_hot((a // 32 == b // 256) & (a % 32 == (b % 256) // 8))
    a, b = iota((32, 128), 0), iota((32, 128), 1)
    pick_i = one_hot(a + row * 32 == b)
    pick_j = one_hot(a + (col * sub_count + sub) * 32 == b)
    lane_mask = [one_hot(iota((32, 256), 1) % 8 == g) for g in range(8)]
    ones = jnp.ones((128, 128), BF16)

    for copy in copies:
        copy.wait()

    got_left = recv[:, 0:32].reshape(256, 128)
    by_i = dot(swap_rows, got_left).astype(BF16)
    spread_left = dot(by_i, spread).reshape(32, 8, 1024)
    left_wide[...] = jnp.concatenate(
        [spread_left[:, :, s * 256 : s * 256 + 256] for s in range(4)], axis=1
    ).astype(BF16)
    got_right = [recv[d, 32:64].astype(F32) for d in range(8)]
    stacked = jnp.concatenate(
        [
            jnp.concatenate([g[:, eb * 32 : eb * 32 + 32] for g in got_right], axis=1)
            for eb in range(4)
        ],
        axis=0,
    ).astype(BF16)
    right_rows = dot(stacked, swap_lanes).astype(BF16)
    masks = recv[:, 64:80].reshape(128, 128)
    ml_buf[...] = dot_nt(pick_i, masks)
    mr = dot_nt(pick_j, masks)

    def chunk(step, carry):
        for n in range(8):
            i = step * 8 + n
            base = left_wide[i]
            block = jnp.concatenate([base * m for m in lane_mask], axis=0)
            made = dot(right_rows, block).astype(BF16)
            for eb in range(4):
                prod[eb, n * 32 : n * 32 + 32] = made[eb * 32 : eb * 32 + 32]
            cm_buf[n * 32 : n * 32 + 32] = (ml_buf[pl.ds(i, 1)] * mr).astype(BF16)
        counts = dot(cm_buf[...], ones)
        total = dot(prod[0], w_buf[0])
        for eb in range(1, 4):
            total += dot(prod[eb], w_buf[eb])
        update = (total + oo_ref[...]) / jnp.maximum(counts, 1.0)
        first = pl.multiple_of(step * 8, 8)
        summed = pair_ref[pl.ds(first, 8)].astype(F32).reshape(256, 128) + update
        result = normalize(summed, pg_ref[...], po_ref[...]).astype(BF16)
        out_ref[pl.ds(first, 8)] = result.reshape(8, 32, 128)
        return carry

    lax.fori_loop(0, 4, chunk, 0)


def fused_body(
    alignment, alignment_mask, residue_mask, pair_state, alignment_gain, alignment_offset,
    left_weight, left_offset, right_weight, right_offset, out_weight, out_offset,
    pair_gain, pair_offset,
):
    row_count = lax.axis_size("row")
    col_count = lax.axis_size("col")
    sub_count = lax.axis_size("sub")
    peers = row_count * col_count
    vmem = pl.BlockSpec(memory_space=pltpu.VMEM)
    return pl.pallas_call(
        functools.partial(pair_kernel, row_count, col_count, sub_count),
        out_shape=jax.ShapeDtypeStruct(pair_state.shape, BF16),
        in_specs=[vmem] * 14,
        out_specs=vmem,
        scratch_shapes=[
            pltpu.VMEM((peers, 80, 128), BF16),
            pltpu.VMEM((peers, 80, 128), BF16),
            pltpu.VMEM((128, 128), BF16),
            pltpu.VMEM((32, 32, 256), BF16),
            pltpu.VMEM((4, 256, 128), BF16),
            pltpu.VMEM((4, 256, 256), BF16),
            pltpu.VMEM((32, 128), F32),
            pltpu.VMEM((256, 128), BF16),
            pltpu.SemaphoreType.DMA((peers,)),
            pltpu.SemaphoreType.DMA((peers,)),
        ],
        compiler_params=pltpu.CompilerParams(
            collective_id=0, has_side_effects=True, vmem_limit_bytes=40 * 2**20
        ),
    )(
        alignment, alignment_mask, residue_mask[None], pair_state,
        alignment_gain[None], alignment_offset[None],
        left_weight, left_offset[None], right_weight, right_offset[None],
        out_weight, out_offset[None], pair_gain[None], pair_offset[None],
    )


def fits(alignment, pair_state):
    senders = lax.axis_size("row") * lax.axis_size("col")
    return senders == 8 and alignment.shape == (4, 128, 256) and pair_state.shape == (32, 32, 128)


def choose(*arrays):
    return (fused_body if fits(arrays[0], arrays[3]) else body)(*arrays)


def solution(mesh):
    placed = (
        P(("groups", "row", "col"), None, None),
        P(("groups", "row", "col"), None),
        P("groups"),
        P(("groups", "row"), ("col", "sub"), None),
        P(),
        P(),
        P(),
        P(),
        P(),
        P(),
        P(),
        P(),
        P(),
        P(),
    )
    return jax.shard_map(
        choose,
        mesh=mesh,
        in_specs=placed,
        out_specs=P(("groups", "row"), ("col", "sub"), None),
        check_vma=False,
    )
```

```python
import functools

import jax
import jax.numpy as jnp
from jax import lax
from jax.experimental import pallas as pl
from jax.experimental.pallas import tpu as pltpu
from jax.sharding import PartitionSpec as P


def normalize(values, scales, offsets):
    average = jnp.mean(values, axis=-1, keepdims=True)
    variance = jnp.mean(values * values, axis=-1, keepdims=True) - average * average
    return (values - average) * lax.rsqrt(variance + 1e-05) * scales + offsets


def project_side(normed, weight, offsets, factor):
    leading = normed.shape[:-1]
    flattened = jnp.dot(
        normed.reshape(-1, normed.shape[-1]), weight, preferred_element_type=jnp.float32
    )
    return ((flattened.reshape(leading + (weight.shape[1],)) + offsets) * factor[..., None]).astype(
        jnp.bfloat16
    )


def reorder(values, row_count, col_count, sub_count):
    local_seqs = values.shape[0]
    portion = values.shape[1] // (row_count * col_count * sub_count)
    trailing = values.shape[2:]
    grouped = values.reshape((local_seqs, col_count, sub_count, row_count, portion) + trailing)
    extra = tuple(range(5, 5 + len(trailing)))
    return jnp.transpose(grouped, (0, 3, 1, 2, 4) + extra).reshape(values.shape)


def own_half(values, sub_count, sub_index):
    sequences = values.shape[0]
    share = values.shape[1] // sub_count
    split = values.reshape((sequences, sub_count, share) + values.shape[2:])
    picked = lax.dynamic_slice_in_dim(split, sub_index, 1, 1)
    return picked.reshape((sequences, share) + values.shape[2:])


def column_terms(left_rows, row_mask, right_cols, col_mask, out_flat, out_offset):
    col_total = right_cols.shape[1]
    results = []
    for first_col in range(0, col_total, 32):
        last_col = min(first_col + 32, col_total)
        selected = right_cols[:, first_col:last_col]
        products = jnp.einsum(
            "sic,sje->ijce", left_rows, selected, preferred_element_type=jnp.float32
        ).astype(jnp.bfloat16)
        pair_rows = products.shape[0] * products.shape[1]
        projected = jnp.dot(
            products.reshape(pair_rows, -1), out_flat, preferred_element_type=jnp.float32
        )
        projected = projected.reshape(products.shape[0], products.shape[1], -1) + out_offset
        counts = jnp.dot(
            row_mask.T, col_mask[:, first_col:last_col], preferred_element_type=jnp.float32
        )
        results.append(projected / jnp.maximum(counts, 1.0)[:, :, None])
    return jnp.concatenate(results, axis=1)


def body(
    alignment,
    alignment_mask,
    residue_mask,
    pair_state,
    alignment_gain,
    alignment_offset,
    left_weight,
    left_offset,
    right_weight,
    right_offset,
    out_weight,
    out_offset,
    pair_gain,
    pair_offset,
):
    row_count = lax.axis_size("row")
    col_count = lax.axis_size("col")
    sub_count = lax.axis_size("sub")
    sub_index = lax.axis_index("sub")
    local_seqs, residues, channels = alignment.shape
    hidden = left_weight.shape[1]
    portion = residues // (row_count * col_count)
    present = (alignment_mask * residue_mask[None, :]).astype(jnp.bfloat16)
    normed = normalize(alignment.astype(jnp.float32), alignment_gain, alignment_offset).astype(
        jnp.bfloat16
    )
    factor = present.astype(jnp.float32)
    left_local = project_side(normed, left_weight, left_offset, factor)
    right_local = reorder(
        project_side(normed, right_weight, right_offset, factor), row_count, col_count, sub_count
    )
    outgoing = (
        left_local.reshape(local_seqs, -1),
        right_local.reshape(local_seqs, -1),
        present,
        reorder(present, row_count, col_count, sub_count),
    )
    arrived = (
        lax.all_to_all(outgoing[0], ("row", "col"), split_axis=1, concat_axis=0, tiled=True),
        lax.all_to_all(outgoing[1], ("row", "col"), split_axis=1, concat_axis=0, tiled=True),
        lax.all_to_all(outgoing[2], ("row", "col"), split_axis=1, concat_axis=0, tiled=True),
        lax.all_to_all(outgoing[3], ("row", "col"), split_axis=1, concat_axis=0, tiled=True),
    )
    sequences = arrived[2].shape[0]
    left_part = arrived[0].reshape(sequences, portion, hidden)
    right_part = own_half(arrived[1].reshape(sequences, portion, hidden), sub_count, sub_index)
    mask_here = arrived[2]
    mask_there = own_half(arrived[3], sub_count, sub_index)
    gathered_rows, row_mask = (
        lax.all_gather(left_part.reshape(sequences, -1), "col", axis=1, tiled=True),
        lax.all_gather(mask_here, "col", axis=1, tiled=True),
    )
    left_rows = gathered_rows.reshape(sequences, -1, hidden)
    out_flat = out_weight.reshape(hidden * hidden, -1)
    pieces = lax.all_gather((right_part, mask_there), "row", axis=1, tiled=True)
    update = column_terms(left_rows, row_mask, pieces[0], pieces[1], out_flat, out_offset)
    summed = pair_state.astype(jnp.float32) + update
    return normalize(summed, pair_gain, pair_offset).astype(jnp.bfloat16)


F32, BF16 = jnp.float32, jnp.bfloat16


def iota(shape, axis):
    return lax.broadcasted_iota(jnp.int32, shape, axis)


def one_hot(condition, kind=BF16):
    return jnp.where(condition, 1.0, 0.0).astype(kind)


def dot(a, b, **options):
    return jnp.dot(a, b, preferred_element_type=F32, **options)


def dot_nt(a, b):
    return lax.dot_general(a, b, (((1,), (1,)), ((), ())), preferred_element_type=F32)


def dot_tn(a, b):
    return lax.dot_general(a, b, (((0,), (0,)), ((), ())), preferred_element_type=F32)


def pair_kernel(
    row_count, col_count, sub_count,
    x_hbm, am_hbm, rm_hbm, ag_hbm, ao_hbm, lw_hbm, lo_hbm, rw_hbm, ro_hbm, ow_hbm, pair_hbm,
    oo_hbm, pg_hbm, po_hbm, out_ref,
    x_ref, am_ref, rm_ref, ag_ref, ao_ref, lw_ref, lo_ref, rw_ref, ro_ref, ow_ref,
    pair_ref, oo_ref, pg_ref, po_ref, left_wide, ml_buf, w_buf, prod, cm_buf,
    send, recv, right_buf, send_sem, recv_sem, load_sem, seq_sem,
):
    peers = row_count * col_count
    row, col, sub = lax.axis_index("row"), lax.axis_index("col"), lax.axis_index("sub")
    me = row * col_count + col
    small = [
        pltpu.make_async_copy(source, target, load_sem.at[n])
        for n, (source, target) in enumerate(
            [
                (lw_hbm, lw_ref), (rw_hbm, rw_ref), (lo_hbm, lo_ref), (ro_hbm, ro_ref),
                (am_hbm, am_ref), (rm_hbm, rm_ref), (ag_hbm, ag_ref), (ao_hbm, ao_ref),
                (ow_hbm, ow_ref), (pair_hbm, pair_ref),
                (oo_hbm, oo_ref), (pg_hbm, pg_ref), (po_hbm, po_ref),
            ]
        )
    ]
    seqs = [pltpu.make_async_copy(x_hbm.at[s], x_ref.at[s], seq_sem.at[s]) for s in range(4)]
    for copy in small[:8] + seqs + small[8:]:
        copy.start()
    barrier = pltpu.get_barrier_semaphore()
    others = []
    for k in range(1, peers):
        peer = lax.rem(me + k, peers)
        place = {"row": peer // col_count, "col": lax.rem(peer, col_count)}
        others.append((k, peer, place))
        pl.semaphore_signal(barrier, inc=1, device_id=place, device_id_type=pl.DeviceIdType.MESH)

    in_32, lane = iota((32, 128), 0), iota((32, 128), 1)
    rep_left = lane % 32 == in_32
    rep_right = (lane // 32) * 8 + lane % 8 == in_32
    at = iota((256, 128), 0)
    seq_row = jnp.where(at < 128, at // 32, (at // 8) % 4)
    eye = one_hot(iota((128, 128), 0) == iota((128, 128), 1))
    lane2 = iota((128, 256), 1)
    seq_lane = jnp.where(lane2 < 128, lane2 // 32, (lane2 // 8) % 4)
    exact = lax.Precision.HIGHEST
    for copy in small[:8]:
        copy.wait()
    wide = jnp.concatenate(
        [dot_tn(lw_ref[...], one_hot(rep_left)), dot_tn(rw_ref[...], one_hot(rep_right))], axis=1
    ).astype(BF16)
    bias = jnp.concatenate(
        [
            dot(jnp.broadcast_to(lo_ref[...], (8, 32)), one_hot(rep_left, F32), precision=exact),
            dot(jnp.broadcast_to(ro_ref[...], (8, 32)), one_hot(rep_right, F32), precision=exact),
        ],
        axis=1,
    )[0:1]
    present = (am_ref[...] * rm_ref[...]).astype(F32)
    mask_rows = jnp.zeros((256, 128), F32)
    for s in range(4):
        mask_rows = jnp.where(seq_row == s, present[s : s + 1], mask_rows)
    mask_here = dot_nt(eye, mask_rows.astype(BF16))
    sides = jnp.zeros((128, 256), F32)
    for s in range(4):
        seqs[s].wait()
        normed = normalize(x_ref[s].astype(F32), ag_ref[...], ao_ref[...]).astype(BF16)
        sides = jnp.where(seq_lane == s, dot(normed, wide), sides)
    sides = ((sides + bias) * mask_here).astype(BF16)
    left = sides[:, :128]
    right_buf[...] = sides[:, 128:]
    mask_block = jnp.concatenate([present, jnp.zeros((12, 128), F32)], axis=0).astype(BF16)
    for d in range(peers):
        r, q = d // col_count, d % col_count
        send[d, 0:32] = left[r * 32 : r * 32 + 32]
        start = pl.multiple_of((q * sub_count + sub) * 32, 32)
        send[d, 32:64] = right_buf[pl.ds(start, 32)]
        send[d, 64:80] = mask_block

    pl.semaphore_wait(barrier, peers - 1)
    copies = []
    for k, peer, place in others:
        copy = pltpu.make_async_remote_copy(
            src_ref=send.at[peer],
            dst_ref=recv.at[me],
            send_sem=send_sem.at[k],
            recv_sem=recv_sem.at[k],
            device_id=place,
            device_id_type=pl.DeviceIdType.MESH,
        )
        copy.start()
        copies.append(copy)
    recv[me] = send[me]

    for copy in small[8:]:
        copy.wait()
    for eb in range(4):
        part = ow_ref[...].astype(F32)[:, eb * 8 : eb * 8 + 8, :]
        w_buf[eb] = part.reshape(256, 128).astype(BF16)
    a, b = iota((256, 256), 0), iota((256, 256), 1)
    swap_rows = one_hot((a % 8 == b // 32) & (a // 8 == b % 32))
    swap_lanes = one_hot((a // 32 == b % 8) & ((a // 8) % 4 == (b // 8) % 4) & (a % 8 == b // 32))
    a, b = iota((128, 1024), 0), iota((128, 1024), 1)
    spread = one_hot((a // 32 == b // 256) & (a % 32 == (b % 256) // 8))
    a, b = iota((32, 128), 0), iota((32, 128), 1)
    pick_i = one_hot(a + row * 32 == b)
    pick_j = one_hot(a + (col * sub_count + sub) * 32 == b)
    lane_mask = [one_hot(iota((32, 256), 1) % 8 == g) for g in range(8)]
    ones = jnp.ones((128, 128), BF16)

    for copy in copies:
        copy.wait()

    got_left = recv[:, 0:32].reshape(256, 128)
    by_i = dot(swap_rows, got_left).astype(BF16)
    spread_left = dot(by_i, spread).reshape(32, 8, 1024)
    left_wide[...] = jnp.concatenate(
        [spread_left[:, :, s * 256 : s * 256 + 256] for s in range(4)], axis=1
    ).astype(BF16)
    got_right = [recv[d, 32:64].astype(F32) for d in range(8)]
    stacked = jnp.concatenate(
        [
            jnp.concatenate([g[:, eb * 32 : eb * 32 + 32] for g in got_right], axis=1)
            for eb in range(4)
        ],
        axis=0,
    ).astype(BF16)
    right_rows = dot(stacked, swap_lanes).astype(BF16)
    masks = recv[:, 64:80].reshape(128, 128)
    ml_buf[...] = dot_nt(pick_i, masks)
    mr = dot_nt(pick_j, masks)

    for step in range(4):
        for n in range(8):
            i = step * 8 + n
            base = left_wide[i]
            block = jnp.concatenate([base * m for m in lane_mask], axis=0)
            made = dot(right_rows, block).astype(BF16)
            for eb in range(4):
                prod[step, eb, n * 32 : n * 32 + 32] = made[eb * 32 : eb * 32 + 32]
            cm_buf[step, n * 32 : n * 32 + 32] = (ml_buf[i : i + 1] * mr).astype(BF16)
        counts = dot(cm_buf[step], ones)
        total = dot(prod[step, 0], w_buf[0])
        for eb in range(1, 4):
            total += dot(prod[step, eb], w_buf[eb])
        update = (total + oo_ref[...]) / jnp.maximum(counts, 1.0)
        rows = pl.ds(step * 8, 8)
        summed = pair_ref[rows].astype(F32).reshape(256, 128) + update
        result = normalize(summed, pg_ref[...], po_ref[...]).astype(BF16)
        out_ref[rows] = result.reshape(8, 32, 128)


def fused_body(
    alignment, alignment_mask, residue_mask, pair_state, alignment_gain, alignment_offset,
    left_weight, left_offset, right_weight, right_offset, out_weight, out_offset,
    pair_gain, pair_offset,
):
    row_count = lax.axis_size("row")
    col_count = lax.axis_size("col")
    sub_count = lax.axis_size("sub")
    peers = row_count * col_count
    vmem = pl.BlockSpec(memory_space=pltpu.VMEM)
    hbm = pl.BlockSpec(memory_space=pltpu.HBM)
    held = (
        alignment, alignment_mask, residue_mask[None],
        alignment_gain[None], alignment_offset[None],
        left_weight.T, left_offset[None], right_weight.T, right_offset[None], out_weight,
        pair_state, out_offset[None], pair_gain[None], pair_offset[None],
    )
    return pl.pallas_call(
        functools.partial(pair_kernel, row_count, col_count, sub_count),
        out_shape=jax.ShapeDtypeStruct(pair_state.shape, BF16),
        in_specs=[hbm] * 14,
        out_specs=vmem,
        scratch_shapes=[pltpu.VMEM(a.shape, a.dtype) for a in held]
        + [
            pltpu.VMEM((32, 32, 256), BF16),
            pltpu.VMEM((32, 128), F32),
            pltpu.VMEM((4, 256, 128), BF16),
            pltpu.VMEM((4, 4, 256, 256), BF16),
            pltpu.VMEM((4, 256, 128), BF16),
            pltpu.VMEM((peers, 80, 128), BF16),
            pltpu.VMEM((peers, 80, 128), BF16),
            pltpu.VMEM((128, 128), BF16),
            pltpu.SemaphoreType.DMA((peers,)),
            pltpu.SemaphoreType.DMA((peers,)),
            pltpu.SemaphoreType.DMA((13,)),
            pltpu.SemaphoreType.DMA((4,)),
        ],
        compiler_params=pltpu.CompilerParams(
            collective_id=0, has_side_effects=True, vmem_limit_bytes=40 * 2**20
        ),
    )(*(pltpu.with_memory_space_constraint(a, pltpu.HBM) for a in held))


def fits(alignment, pair_state):
    senders = lax.axis_size("row") * lax.axis_size("col")
    return senders == 8 and alignment.shape == (4, 128, 256) and pair_state.shape == (32, 32, 128)


def choose(*arrays):
    return (fused_body if fits(arrays[0], arrays[3]) else body)(*arrays)


def solution(mesh):
    placed = (
        P(("groups", "row", "col"), None, None),
        P(("groups", "row", "col"), None),
        P("groups"),
        P(("groups", "row"), ("col", "sub"), None),
        P(),
        P(),
        P(),
        P(),
        P(),
        P(),
        P(),
        P(),
        P(),
        P(),
    )
    return jax.shard_map(
        choose,
        mesh=mesh,
        in_specs=placed,
        out_specs=P(("groups", "row"), ("col", "sub"), None),
        check_vma=False,
    )
```

```python
import functools

import jax
import jax.numpy as jnp
from jax import lax
from jax.experimental import pallas as pl
from jax.experimental.pallas import tpu as pltpu
from jax.sharding import PartitionSpec as P


def normalize(values, scales, offsets):
    average = jnp.mean(values, axis=-1, keepdims=True)
    variance = jnp.mean(values * values, axis=-1, keepdims=True) - average * average
    return (values - average) * lax.rsqrt(variance + 1e-05) * scales + offsets


def project_side(normed, weight, offsets, factor):
    leading = normed.shape[:-1]
    flattened = jnp.dot(
        normed.reshape(-1, normed.shape[-1]), weight, preferred_element_type=jnp.float32
    )
    return ((flattened.reshape(leading + (weight.shape[1],)) + offsets) * factor[..., None]).astype(
        jnp.bfloat16
    )


def reorder(values, row_count, col_count, sub_count):
    local_seqs = values.shape[0]
    portion = values.shape[1] // (row_count * col_count * sub_count)
    trailing = values.shape[2:]
    grouped = values.reshape((local_seqs, col_count, sub_count, row_count, portion) + trailing)
    extra = tuple(range(5, 5 + len(trailing)))
    return jnp.transpose(grouped, (0, 3, 1, 2, 4) + extra).reshape(values.shape)


def own_half(values, sub_count, sub_index):
    sequences = values.shape[0]
    share = values.shape[1] // sub_count
    split = values.reshape((sequences, sub_count, share) + values.shape[2:])
    picked = lax.dynamic_slice_in_dim(split, sub_index, 1, 1)
    return picked.reshape((sequences, share) + values.shape[2:])


def column_terms(left_rows, row_mask, right_cols, col_mask, out_flat, out_offset):
    col_total = right_cols.shape[1]
    results = []
    for first_col in range(0, col_total, 32):
        last_col = min(first_col + 32, col_total)
        selected = right_cols[:, first_col:last_col]
        products = jnp.einsum(
            "sic,sje->ijce", left_rows, selected, preferred_element_type=jnp.float32
        ).astype(jnp.bfloat16)
        pair_rows = products.shape[0] * products.shape[1]
        projected = jnp.dot(
            products.reshape(pair_rows, -1), out_flat, preferred_element_type=jnp.float32
        )
        projected = projected.reshape(products.shape[0], products.shape[1], -1) + out_offset
        counts = jnp.dot(
            row_mask.T, col_mask[:, first_col:last_col], preferred_element_type=jnp.float32
        )
        results.append(projected / jnp.maximum(counts, 1.0)[:, :, None])
    return jnp.concatenate(results, axis=1)


def body(
    alignment,
    alignment_mask,
    residue_mask,
    pair_state,
    alignment_gain,
    alignment_offset,
    left_weight,
    left_offset,
    right_weight,
    right_offset,
    out_weight,
    out_offset,
    pair_gain,
    pair_offset,
):
    row_count = lax.axis_size("row")
    col_count = lax.axis_size("col")
    sub_count = lax.axis_size("sub")
    sub_index = lax.axis_index("sub")
    local_seqs, residues, channels = alignment.shape
    hidden = left_weight.shape[1]
    portion = residues // (row_count * col_count)
    present = (alignment_mask * residue_mask[None, :]).astype(jnp.bfloat16)
    normed = normalize(alignment.astype(jnp.float32), alignment_gain, alignment_offset).astype(
        jnp.bfloat16
    )
    factor = present.astype(jnp.float32)
    left_local = project_side(normed, left_weight, left_offset, factor)
    right_local = reorder(
        project_side(normed, right_weight, right_offset, factor), row_count, col_count, sub_count
    )
    outgoing = (
        left_local.reshape(local_seqs, -1),
        right_local.reshape(local_seqs, -1),
        present,
        reorder(present, row_count, col_count, sub_count),
    )
    arrived = (
        lax.all_to_all(outgoing[0], ("row", "col"), split_axis=1, concat_axis=0, tiled=True),
        lax.all_to_all(outgoing[1], ("row", "col"), split_axis=1, concat_axis=0, tiled=True),
        lax.all_to_all(outgoing[2], ("row", "col"), split_axis=1, concat_axis=0, tiled=True),
        lax.all_to_all(outgoing[3], ("row", "col"), split_axis=1, concat_axis=0, tiled=True),
    )
    sequences = arrived[2].shape[0]
    left_part = arrived[0].reshape(sequences, portion, hidden)
    right_part = own_half(arrived[1].reshape(sequences, portion, hidden), sub_count, sub_index)
    mask_here = arrived[2]
    mask_there = own_half(arrived[3], sub_count, sub_index)
    gathered_rows, row_mask = (
        lax.all_gather(left_part.reshape(sequences, -1), "col", axis=1, tiled=True),
        lax.all_gather(mask_here, "col", axis=1, tiled=True),
    )
    left_rows = gathered_rows.reshape(sequences, -1, hidden)
    out_flat = out_weight.reshape(hidden * hidden, -1)
    pieces = lax.all_gather((right_part, mask_there), "row", axis=1, tiled=True)
    update = column_terms(left_rows, row_mask, pieces[0], pieces[1], out_flat, out_offset)
    summed = pair_state.astype(jnp.float32) + update
    return normalize(summed, pair_gain, pair_offset).astype(jnp.bfloat16)


F32, BF16 = jnp.float32, jnp.bfloat16


def iota(shape, axis):
    return lax.broadcasted_iota(jnp.int32, shape, axis)


def one_hot(condition, kind=BF16):
    return jnp.where(condition, 1.0, 0.0).astype(kind)


def dot(a, b, **options):
    return jnp.dot(a, b, preferred_element_type=F32, **options)


def dot_nt(a, b):
    return lax.dot_general(a, b, (((1,), (1,)), ((), ())), preferred_element_type=F32)


def dot_tn(a, b):
    return lax.dot_general(a, b, (((0,), (0,)), ((), ())), preferred_element_type=F32)


def pair_kernel(
    row_count, col_count, sub_count,
    x_hbm, am_hbm, rm_hbm, ag_hbm, ao_hbm, lw_hbm, lo_hbm, rw_hbm, ro_hbm, ow_hbm, pair_hbm,
    oo_hbm, pg_hbm, po_hbm, out_ref,
    x_ref, am_ref, rm_ref, ag_ref, ao_ref, lw_ref, lo_ref, rw_ref, ro_ref, ow_ref,
    pair_ref, oo_ref, pg_ref, po_ref, left_wide, ml_buf, w_buf, prod, cm_buf,
    send, recv, right_buf, send_sem, recv_sem, load_sem, seq_sem,
):
    peers = row_count * col_count
    row, col, sub = lax.axis_index("row"), lax.axis_index("col"), lax.axis_index("sub")
    me = row * col_count + col
    small = [
        pltpu.make_async_copy(source, target, load_sem.at[n])
        for n, (source, target) in enumerate(
            [
                (lw_hbm, lw_ref), (rw_hbm, rw_ref), (lo_hbm, lo_ref), (ro_hbm, ro_ref),
                (am_hbm, am_ref), (rm_hbm, rm_ref), (ag_hbm, ag_ref), (ao_hbm, ao_ref),
                (ow_hbm, ow_ref), (pair_hbm, pair_ref),
                (oo_hbm, oo_ref), (pg_hbm, pg_ref), (po_hbm, po_ref),
            ]
        )
    ]
    seqs = [pltpu.make_async_copy(x_hbm.at[s], x_ref.at[s], seq_sem.at[s]) for s in range(4)]
    for copy in small[:8] + seqs + small[8:]:
        copy.start()
    barrier = pltpu.get_barrier_semaphore()
    others = []
    for k in range(1, peers):
        peer = lax.rem(me + k, peers)
        place = {"row": peer // col_count, "col": lax.rem(peer, col_count)}
        others.append((k, peer, place))
        pl.semaphore_signal(barrier, inc=1, device_id=place, device_id_type=pl.DeviceIdType.MESH)

    in_32, lane = iota((32, 128), 0), iota((32, 128), 1)
    rep_left = lane % 32 == in_32
    rep_right = (lane // 32) * 8 + lane % 8 == in_32
    at = iota((256, 128), 0)
    seq_row = jnp.where(at < 128, at // 32, (at // 8) % 4)
    eye = one_hot(iota((128, 128), 0) == iota((128, 128), 1))
    lane2 = iota((128, 256), 1)
    seq_lane = jnp.where(lane2 < 128, lane2 // 32, (lane2 // 8) % 4)
    for copy in small[:8] + seqs:
        copy.wait()
    wide = jnp.concatenate(
        [dot_tn(lw_ref[...], one_hot(rep_left)), dot_tn(rw_ref[...], one_hot(rep_right))], axis=1
    ).astype(BF16)
    bias = jnp.concatenate(
        [lo_ref[...]] * 4
        + [ro_ref[:, eb * 8 : eb * 8 + 8] for eb in range(4) for s in range(4)],
        axis=1,
    )
    present = (am_ref[...] * rm_ref[...]).astype(F32)
    mask_rows = jnp.zeros((256, 128), F32)
    for s in range(4):
        mask_rows = jnp.where(seq_row == s, present[s : s + 1], mask_rows)
    mask_here = dot_nt(eye, mask_rows.astype(BF16))
    sides = jnp.zeros((128, 256), F32)
    for s in range(4):
        normed = normalize(x_ref[s].astype(F32), ag_ref[...], ao_ref[...]).astype(BF16)
        sides = jnp.where(seq_lane == s, dot(normed, wide), sides)
    sides = ((sides + bias) * mask_here).astype(BF16)
    left = sides[:, :128]
    right_buf[...] = sides[:, 128:]
    mask_block = jnp.concatenate([present, jnp.zeros((12, 128), F32)], axis=0).astype(BF16)
    for d in range(peers):
        r, q = d // col_count, d % col_count
        send[d, 0:32] = left[r * 32 : r * 32 + 32]
        start = pl.multiple_of((q * sub_count + sub) * 32, 32)
        send[d, 32:64] = right_buf[pl.ds(start, 32)]
        send[d, 64:80] = mask_block

    pl.semaphore_wait(barrier, peers - 1)
    copies = []
    for k, peer, place in others:
        copy = pltpu.make_async_remote_copy(
            src_ref=send.at[peer],
            dst_ref=recv.at[me],
            send_sem=send_sem.at[k],
            recv_sem=recv_sem.at[k],
            device_id=place,
            device_id_type=pl.DeviceIdType.MESH,
        )
        copy.start()
        copies.append(copy)
    recv[me] = send[me]

    for copy in small[8:]:
        copy.wait()
    for eb in range(4):
        part = ow_ref[...].astype(F32)[:, eb * 8 : eb * 8 + 8, :]
        w_buf[eb] = part.reshape(256, 128).astype(BF16)
    a, b = iota((256, 256), 0), iota((256, 256), 1)
    swap_rows = one_hot((a % 8 == b // 32) & (a // 8 == b % 32))
    swap_lanes = one_hot((a // 32 == b % 8) & ((a // 8) % 4 == (b // 8) % 4) & (a % 8 == b // 32))
    a, b = iota((128, 1024), 0), iota((128, 1024), 1)
    spread = one_hot((a // 32 == b // 256) & (a % 32 == (b % 256) // 8))
    a, b = iota((32, 128), 0), iota((32, 128), 1)
    pick_i = one_hot(a + row * 32 == b)
    pick_j = one_hot(a + (col * sub_count + sub) * 32 == b)
    lane_mask = [one_hot(iota((32, 256), 1) % 8 == g) for g in range(8)]
    ones = jnp.ones((128, 128), BF16)

    for copy in copies:
        copy.wait()

    got_left = recv[:, 0:32].reshape(256, 128)
    by_i = dot(swap_rows, got_left).astype(BF16)
    spread_left = dot(by_i, spread).reshape(32, 8, 1024)
    left_wide[...] = jnp.concatenate(
        [spread_left[:, :, s * 256 : s * 256 + 256] for s in range(4)], axis=1
    ).astype(BF16)
    got_right = [recv[d, 32:64].astype(F32) for d in range(8)]
    stacked = jnp.concatenate(
        [
            jnp.concatenate([g[:, eb * 32 : eb * 32 + 32] for g in got_right], axis=1)
            for eb in range(4)
        ],
        axis=0,
    ).astype(BF16)
    right_rows = dot(stacked, swap_lanes).astype(BF16)
    masks = recv[:, 64:80].reshape(128, 128)
    ml_buf[...] = dot_nt(pick_i, masks)
    mr = dot_nt(pick_j, masks)

    for step in range(4):
        for n in range(8):
            i = step * 8 + n
            base = left_wide[i]
            block = jnp.concatenate([base * m for m in lane_mask], axis=0)
            made = dot(right_rows, block).astype(BF16)
            for eb in range(4):
                prod[step, eb, n * 32 : n * 32 + 32] = made[eb * 32 : eb * 32 + 32]
            cm_buf[step, n * 32 : n * 32 + 32] = (ml_buf[i : i + 1] * mr).astype(BF16)
        counts = dot(cm_buf[step], ones)
        total = dot(prod[step, 0], w_buf[0])
        for eb in range(1, 4):
            total += dot(prod[step, eb], w_buf[eb])
        update = (total + oo_ref[...]) / jnp.maximum(counts, 1.0)
        rows = pl.ds(step * 8, 8)
        summed = pair_ref[rows].astype(F32).reshape(256, 128) + update
        result = normalize(summed, pg_ref[...], po_ref[...]).astype(BF16)
        out_ref[rows] = result.reshape(8, 32, 128)


def fused_body(
    alignment, alignment_mask, residue_mask, pair_state, alignment_gain, alignment_offset,
    left_weight, left_offset, right_weight, right_offset, out_weight, out_offset,
    pair_gain, pair_offset,
):
    row_count = lax.axis_size("row")
    col_count = lax.axis_size("col")
    sub_count = lax.axis_size("sub")
    peers = row_count * col_count
    vmem = pl.BlockSpec(memory_space=pltpu.VMEM)
    hbm = pl.BlockSpec(memory_space=pltpu.HBM)
    held = (
        alignment, alignment_mask, residue_mask[None],
        alignment_gain[None], alignment_offset[None],
        left_weight.T, left_offset[None], right_weight.T, right_offset[None], out_weight,
        pair_state, out_offset[None], pair_gain[None], pair_offset[None],
    )
    return pl.pallas_call(
        functools.partial(pair_kernel, row_count, col_count, sub_count),
        out_shape=jax.ShapeDtypeStruct(pair_state.shape, BF16),
        in_specs=[hbm] * 14,
        out_specs=vmem,
        scratch_shapes=[pltpu.VMEM(a.shape, a.dtype) for a in held]
        + [
            pltpu.VMEM((32, 32, 256), BF16),
            pltpu.VMEM((32, 128), F32),
            pltpu.VMEM((4, 256, 128), BF16),
            pltpu.VMEM((4, 4, 256, 256), BF16),
            pltpu.VMEM((4, 256, 128), BF16),
            pltpu.VMEM((peers, 80, 128), BF16),
            pltpu.VMEM((peers, 80, 128), BF16),
            pltpu.VMEM((128, 128), BF16),
            pltpu.SemaphoreType.DMA((peers,)),
            pltpu.SemaphoreType.DMA((peers,)),
            pltpu.SemaphoreType.DMA((13,)),
            pltpu.SemaphoreType.DMA((4,)),
        ],
        compiler_params=pltpu.CompilerParams(
            collective_id=0, has_side_effects=True, vmem_limit_bytes=40 * 2**20
        ),
    )(*(pltpu.with_memory_space_constraint(a, pltpu.HBM) for a in held))


def fits(alignment, pair_state):
    senders = lax.axis_size("row") * lax.axis_size("col")
    return senders == 8 and alignment.shape == (4, 128, 256) and pair_state.shape == (32, 32, 128)


def choose(*arrays):
    return (fused_body if fits(arrays[0], arrays[3]) else body)(*arrays)


def solution(mesh):
    placed = (
        P(("groups", "row", "col"), None, None),
        P(("groups", "row", "col"), None),
        P("groups"),
        P(("groups", "row"), ("col", "sub"), None),
        P(),
        P(),
        P(),
        P(),
        P(),
        P(),
        P(),
        P(),
        P(),
        P(),
    )
    return jax.shard_map(
        choose,
        mesh=mesh,
        in_specs=placed,
        out_specs=P(("groups", "row"), ("col", "sub"), None),
        check_vma=False,
    )
```

```python
import functools

import jax
import jax.numpy as jnp
from jax import lax
from jax.experimental import pallas as pl
from jax.experimental.pallas import tpu as pltpu
from jax.sharding import PartitionSpec as P


def normalize(values, scales, offsets):
    average = jnp.mean(values, axis=-1, keepdims=True)
    variance = jnp.mean(values * values, axis=-1, keepdims=True) - average * average
    return (values - average) * lax.rsqrt(variance + 1e-05) * scales + offsets


def project_side(normed, weight, offsets, factor):
    leading = normed.shape[:-1]
    flattened = jnp.dot(
        normed.reshape(-1, normed.shape[-1]), weight, preferred_element_type=jnp.float32
    )
    return ((flattened.reshape(leading + (weight.shape[1],)) + offsets) * factor[..., None]).astype(
        jnp.bfloat16
    )


def reorder(values, row_count, col_count, sub_count):
    local_seqs = values.shape[0]
    portion = values.shape[1] // (row_count * col_count * sub_count)
    trailing = values.shape[2:]
    grouped = values.reshape((local_seqs, col_count, sub_count, row_count, portion) + trailing)
    extra = tuple(range(5, 5 + len(trailing)))
    return jnp.transpose(grouped, (0, 3, 1, 2, 4) + extra).reshape(values.shape)


def own_half(values, sub_count, sub_index):
    sequences = values.shape[0]
    share = values.shape[1] // sub_count
    split = values.reshape((sequences, sub_count, share) + values.shape[2:])
    picked = lax.dynamic_slice_in_dim(split, sub_index, 1, 1)
    return picked.reshape((sequences, share) + values.shape[2:])


def column_terms(left_rows, row_mask, right_cols, col_mask, out_flat, out_offset):
    col_total = right_cols.shape[1]
    results = []
    for first_col in range(0, col_total, 32):
        last_col = min(first_col + 32, col_total)
        selected = right_cols[:, first_col:last_col]
        products = jnp.einsum(
            "sic,sje->ijce", left_rows, selected, preferred_element_type=jnp.float32
        ).astype(jnp.bfloat16)
        pair_rows = products.shape[0] * products.shape[1]
        projected = jnp.dot(
            products.reshape(pair_rows, -1), out_flat, preferred_element_type=jnp.float32
        )
        projected = projected.reshape(products.shape[0], products.shape[1], -1) + out_offset
        counts = jnp.dot(
            row_mask.T, col_mask[:, first_col:last_col], preferred_element_type=jnp.float32
        )
        results.append(projected / jnp.maximum(counts, 1.0)[:, :, None])
    return jnp.concatenate(results, axis=1)


def body(
    alignment,
    alignment_mask,
    residue_mask,
    pair_state,
    alignment_gain,
    alignment_offset,
    left_weight,
    left_offset,
    right_weight,
    right_offset,
    out_weight,
    out_offset,
    pair_gain,
    pair_offset,
):
    row_count = lax.axis_size("row")
    col_count = lax.axis_size("col")
    sub_count = lax.axis_size("sub")
    sub_index = lax.axis_index("sub")
    local_seqs, residues, channels = alignment.shape
    hidden = left_weight.shape[1]
    portion = residues // (row_count * col_count)
    present = (alignment_mask * residue_mask[None, :]).astype(jnp.bfloat16)
    normed = normalize(alignment.astype(jnp.float32), alignment_gain, alignment_offset).astype(
        jnp.bfloat16
    )
    factor = present.astype(jnp.float32)
    left_local = project_side(normed, left_weight, left_offset, factor)
    right_local = reorder(
        project_side(normed, right_weight, right_offset, factor), row_count, col_count, sub_count
    )
    outgoing = (
        left_local.reshape(local_seqs, -1),
        right_local.reshape(local_seqs, -1),
        present,
        reorder(present, row_count, col_count, sub_count),
    )
    arrived = (
        lax.all_to_all(outgoing[0], ("row", "col"), split_axis=1, concat_axis=0, tiled=True),
        lax.all_to_all(outgoing[1], ("row", "col"), split_axis=1, concat_axis=0, tiled=True),
        lax.all_to_all(outgoing[2], ("row", "col"), split_axis=1, concat_axis=0, tiled=True),
        lax.all_to_all(outgoing[3], ("row", "col"), split_axis=1, concat_axis=0, tiled=True),
    )
    sequences = arrived[2].shape[0]
    left_part = arrived[0].reshape(sequences, portion, hidden)
    right_part = own_half(arrived[1].reshape(sequences, portion, hidden), sub_count, sub_index)
    mask_here = arrived[2]
    mask_there = own_half(arrived[3], sub_count, sub_index)
    gathered_rows, row_mask = (
        lax.all_gather(left_part.reshape(sequences, -1), "col", axis=1, tiled=True),
        lax.all_gather(mask_here, "col", axis=1, tiled=True),
    )
    left_rows = gathered_rows.reshape(sequences, -1, hidden)
    out_flat = out_weight.reshape(hidden * hidden, -1)
    pieces = lax.all_gather((right_part, mask_there), "row", axis=1, tiled=True)
    update = column_terms(left_rows, row_mask, pieces[0], pieces[1], out_flat, out_offset)
    summed = pair_state.astype(jnp.float32) + update
    return normalize(summed, pair_gain, pair_offset).astype(jnp.bfloat16)


F32, BF16 = jnp.float32, jnp.bfloat16


def iota(shape, axis):
    return lax.broadcasted_iota(jnp.int32, shape, axis)


def one_hot(condition, kind=BF16):
    return jnp.where(condition, 1.0, 0.0).astype(kind)


def dot(a, b, **options):
    return jnp.dot(a, b, preferred_element_type=F32, **options)


def dot_nt(a, b):
    return lax.dot_general(a, b, (((1,), (1,)), ((), ())), preferred_element_type=F32)


def dot_tn(a, b):
    return lax.dot_general(a, b, (((0,), (0,)), ((), ())), preferred_element_type=F32)


def pair_kernel(
    row_count, col_count, sub_count,
    x_hbm, am_hbm, rm_hbm, ag_hbm, ao_hbm, lw_hbm, lo_hbm, rw_hbm, ro_hbm, ow_hbm, pair_hbm,
    oo_hbm, pg_hbm, po_hbm, out_ref,
    x_ref, am_ref, rm_ref, ag_ref, ao_ref, lw_ref, lo_ref, rw_ref, ro_ref, ow_ref,
    pair_ref, oo_ref, pg_ref, po_ref, left_wide, ml_buf, w_buf, prod, cm_buf,
    send, recv, right_buf, send_sem, recv_sem, load_sem, seq_sem,
):
    peers = row_count * col_count
    row, col, sub = lax.axis_index("row"), lax.axis_index("col"), lax.axis_index("sub")
    me = row * col_count + col
    small = [
        pltpu.make_async_copy(source, target, load_sem.at[n])
        for n, (source, target) in enumerate(
            [
                (lw_hbm, lw_ref), (rw_hbm, rw_ref), (lo_hbm, lo_ref), (ro_hbm, ro_ref),
                (am_hbm, am_ref), (rm_hbm, rm_ref), (ag_hbm, ag_ref), (ao_hbm, ao_ref),
                (ow_hbm, ow_ref), (pair_hbm, pair_ref),
                (oo_hbm, oo_ref), (pg_hbm, pg_ref), (po_hbm, po_ref),
            ]
        )
    ]
    seqs = [pltpu.make_async_copy(x_hbm.at[s], x_ref.at[s], seq_sem.at[s]) for s in range(4)]
    for copy in small[:8] + seqs + small[8:]:
        copy.start()
    barrier = pltpu.get_barrier_semaphore()
    others = []
    for k in range(1, peers):
        peer = lax.rem(me + k, peers)
        place = {"row": peer // col_count, "col": lax.rem(peer, col_count)}
        others.append((k, peer, place))
        pl.semaphore_signal(barrier, inc=1, device_id=place, device_id_type=pl.DeviceIdType.MESH)

    in_32, lane = iota((32, 128), 0), iota((32, 128), 1)
    rep_left = lane % 32 == in_32
    rep_right = (lane // 32) * 8 + lane % 8 == in_32
    at = iota((256, 128), 0)
    seq_row = jnp.where(at < 128, at // 32, (at // 8) % 4)
    eye = one_hot(iota((128, 128), 0) == iota((128, 128), 1))
    lane2 = iota((128, 256), 1)
    seq_lane = jnp.where(lane2 < 128, lane2 // 32, (lane2 // 8) % 4)
    for copy in small[:8] + seqs:
        copy.wait()
    wide = jnp.concatenate(
        [dot_tn(lw_ref[...], one_hot(rep_left)), dot_tn(rw_ref[...], one_hot(rep_right))], axis=1
    ).astype(BF16)
    bias = jnp.concatenate(
        [lo_ref[...]] * 4
        + [ro_ref[:, eb * 8 : eb * 8 + 8] for eb in range(4) for s in range(4)],
        axis=1,
    )
    present = (am_ref[...] * rm_ref[...]).astype(F32)
    mask_rows = jnp.zeros((256, 128), F32)
    for s in range(4):
        mask_rows = jnp.where(seq_row == s, present[s : s + 1], mask_rows)
    mask_here = dot_nt(eye, mask_rows.astype(BF16))
    all_ones = jnp.ones((256, 128), BF16)
    sides = jnp.zeros((128, 256), F32)
    for s in range(4):
        values = x_ref[s].astype(F32)
        squares = values * values
        high = squares.astype(BF16)
        low = (squares - high.astype(F32)).astype(BF16)
        average = dot(x_ref[s], all_ones) * (1.0 / 256)
        scale = (dot(high, all_ones) + dot(low, all_ones)) * (1.0 / 256) - average * average
        scale = lax.rsqrt(scale + 1e-05)
        average, scale = (jnp.concatenate([v, v], axis=1) for v in (average, scale))
        normed = ((values - average) * scale * ag_ref[...] + ao_ref[...]).astype(BF16)
        sides = jnp.where(seq_lane == s, dot(normed, wide), sides)
    sides = ((sides + bias) * mask_here).astype(BF16)
    left = sides[:, :128]
    right_buf[...] = sides[:, 128:]
    mask_block = jnp.concatenate([present, jnp.zeros((12, 128), F32)], axis=0).astype(BF16)
    for d in range(peers):
        r, q = d // col_count, d % col_count
        send[d, 0:32] = left[r * 32 : r * 32 + 32]
        start = pl.multiple_of((q * sub_count + sub) * 32, 32)
        send[d, 32:64] = right_buf[pl.ds(start, 32)]
        send[d, 64:80] = mask_block

    pl.semaphore_wait(barrier, peers - 1)
    copies = []
    for k, peer, place in others:
        copy = pltpu.make_async_remote_copy(
            src_ref=send.at[peer],
            dst_ref=recv.at[me],
            send_sem=send_sem.at[k],
            recv_sem=recv_sem.at[k],
            device_id=place,
            device_id_type=pl.DeviceIdType.MESH,
        )
        copy.start()
        copies.append(copy)
    recv[me] = send[me]

    for copy in small[8:]:
        copy.wait()
    for eb in range(4):
        part = ow_ref[...].astype(F32)[:, eb * 8 : eb * 8 + 8, :]
        w_buf[eb] = part.reshape(256, 128).astype(BF16)
    a, b = iota((256, 256), 0), iota((256, 256), 1)
    swap_rows = one_hot((a % 8 == b // 32) & (a // 8 == b % 32))
    swap_lanes = one_hot((a // 32 == b % 8) & ((a // 8) % 4 == (b // 8) % 4) & (a % 8 == b // 32))
    a, b = iota((128, 1024), 0), iota((128, 1024), 1)
    spread = one_hot((a // 32 == b // 256) & (a % 32 == (b % 256) // 8))
    a, b = iota((32, 128), 0), iota((32, 128), 1)
    pick_i = one_hot(a + row * 32 == b)
    pick_j = one_hot(a + (col * sub_count + sub) * 32 == b)
    lane_mask = [one_hot(iota((32, 256), 1) % 8 == g) for g in range(8)]
    ones = jnp.ones((128, 128), BF16)

    for copy in copies:
        copy.wait()

    got_left = recv[:, 0:32].reshape(256, 128)
    by_i = dot(swap_rows, got_left).astype(BF16)
    spread_left = dot(by_i, spread).reshape(32, 8, 1024)
    left_wide[...] = jnp.concatenate(
        [spread_left[:, :, s * 256 : s * 256 + 256] for s in range(4)], axis=1
    ).astype(BF16)
    got_right = [recv[d, 32:64].astype(F32) for d in range(8)]
    stacked = jnp.concatenate(
        [
            jnp.concatenate([g[:, eb * 32 : eb * 32 + 32] for g in got_right], axis=1)
            for eb in range(4)
        ],
        axis=0,
    ).astype(BF16)
    right_rows = dot(stacked, swap_lanes).astype(BF16)
    masks = recv[:, 64:80].reshape(128, 128)
    ml_buf[...] = dot_nt(pick_i, masks)
    mr = dot_nt(pick_j, masks)

    for step in range(4):
        for n in range(8):
            i = step * 8 + n
            base = left_wide[i]
            block = jnp.concatenate([base * m for m in lane_mask], axis=0)
            made = dot(right_rows, block).astype(BF16)
            for eb in range(4):
                prod[step, eb, n * 32 : n * 32 + 32] = made[eb * 32 : eb * 32 + 32]
            cm_buf[step, n * 32 : n * 32 + 32] = (ml_buf[i : i + 1] * mr).astype(BF16)
        counts = dot(cm_buf[step], ones)
        total = dot(prod[step, 0], w_buf[0])
        for eb in range(1, 4):
            total += dot(prod[step, eb], w_buf[eb])
        update = (total + oo_ref[...]) / jnp.maximum(counts, 1.0)
        rows = pl.ds(step * 8, 8)
        summed = pair_ref[rows].astype(F32).reshape(256, 128) + update
        result = normalize(summed, pg_ref[...], po_ref[...]).astype(BF16)
        out_ref[rows] = result.reshape(8, 32, 128)


def fused_body(
    alignment, alignment_mask, residue_mask, pair_state, alignment_gain, alignment_offset,
    left_weight, left_offset, right_weight, right_offset, out_weight, out_offset,
    pair_gain, pair_offset,
):
    row_count = lax.axis_size("row")
    col_count = lax.axis_size("col")
    sub_count = lax.axis_size("sub")
    peers = row_count * col_count
    vmem = pl.BlockSpec(memory_space=pltpu.VMEM)
    hbm = pl.BlockSpec(memory_space=pltpu.HBM)
    held = (
        alignment, alignment_mask, residue_mask[None],
        alignment_gain[None], alignment_offset[None],
        left_weight.T, left_offset[None], right_weight.T, right_offset[None], out_weight,
        pair_state, out_offset[None], pair_gain[None], pair_offset[None],
    )
    return pl.pallas_call(
        functools.partial(pair_kernel, row_count, col_count, sub_count),
        out_shape=jax.ShapeDtypeStruct(pair_state.shape, BF16),
        in_specs=[hbm] * 14,
        out_specs=vmem,
        scratch_shapes=[pltpu.VMEM(a.shape, a.dtype) for a in held]
        + [
            pltpu.VMEM((32, 32, 256), BF16),
            pltpu.VMEM((32, 128), F32),
            pltpu.VMEM((4, 256, 128), BF16),
            pltpu.VMEM((4, 4, 256, 256), BF16),
            pltpu.VMEM((4, 256, 128), BF16),
            pltpu.VMEM((peers, 80, 128), BF16),
            pltpu.VMEM((peers, 80, 128), BF16),
            pltpu.VMEM((128, 128), BF16),
            pltpu.SemaphoreType.DMA((peers,)),
            pltpu.SemaphoreType.DMA((peers,)),
            pltpu.SemaphoreType.DMA((13,)),
            pltpu.SemaphoreType.DMA((4,)),
        ],
        compiler_params=pltpu.CompilerParams(
            collective_id=0, has_side_effects=True, vmem_limit_bytes=40 * 2**20
        ),
    )(*(pltpu.with_memory_space_constraint(a, pltpu.HBM) for a in held))


def fits(alignment, pair_state):
    senders = lax.axis_size("row") * lax.axis_size("col")
    return senders == 8 and alignment.shape == (4, 128, 256) and pair_state.shape == (32, 32, 128)


def choose(*arrays):
    return (fused_body if fits(arrays[0], arrays[3]) else body)(*arrays)


def solution(mesh):
    placed = (
        P(("groups", "row", "col"), None, None),
        P(("groups", "row", "col"), None),
        P("groups"),
        P(("groups", "row"), ("col", "sub"), None),
        P(),
        P(),
        P(),
        P(),
        P(),
        P(),
        P(),
        P(),
        P(),
        P(),
    )
    return jax.shard_map(
        choose,
        mesh=mesh,
        in_specs=placed,
        out_specs=P(("groups", "row"), ("col", "sub"), None),
        check_vma=False,
    )
```
